32 devices in a mesh: fiber: 8 (over z, y), group: 4 (over x, core).
Axes of the slice: x: 2, y: 2, z: 4, core: 2. Of those that a mesh axis runs over, the one named last changes fastest.
Arguments:
- tensor_slab: float32 [512, 32, 4096], P('fiber', None, 'group'), may hold values from -168 to 168
- start_matrix: float32 [512, 128], replicated, may hold values from -6 to 6
Outputs:
- triangle: float32 [512, 512], replicated
- subspace_basis: float32 [512, 128], replicated
- core_tensor: float32 [128, 32, 4096], P(None, 'fiber', 'group')
The draws below stay inside these ranges and needn't reach their ends.
All inputs are finite; a program needn't handle non-finite values.
Results may differ from the reference program's by a relative error of at most 0.00016.
Values sent between devices are 32-bit elements; how exact they have to be, the bound alone decides.
A program may use at most 128 MiB of HBM per device.

```python
import jax
import jax.numpy as jnp
from jax import lax

MODE = 512
RANK = 128
ITERS = 2
SL_DEV = 4
CELL_DEV = 1024
SLICES = 32
CELLS = 4096


def draw_tensor_slab(key, part):
    noise_key = jax.random.fold_in(key, 11)
    row_key = jax.random.fold_in(key, 12)
    col_key = jax.random.fold_in(key, 13)
    own_key = jax.random.fold_in(key, 14)
    full_shape = (MODE + 2, SLICES, CELLS)
    noise_field = jax.random.truncated_normal(noise_key, -6.0, 6.0, full_shape, jnp.float32)
    row_scale = jnp.exp(jax.random.uniform(row_key, (MODE,), jnp.float32, 0.0, 0.6931472))
    mixed_field = noise_field[:MODE] + 0.5 * noise_field[1:MODE + 1] + 0.25 * noise_field[2:]
    col_scale = jnp.exp(jax.random.uniform(col_key, (SLICES, CELLS), jnp.float32, -0.6931472, 0.6931472))
    row_order = jax.random.permutation(own_key, MODE)
    devices_all = SLICES // SL_DEV * (CELLS // CELL_DEV)
    row_owner = row_order * devices_all // MODE
    slice_owner = jnp.arange(SLICES) // SL_DEV
    cell_owner = jnp.arange(CELLS) // CELL_DEV
    column_owner = slice_owner[:, None] * (CELLS // CELL_DEV) + cell_owner[None, :]
    spike_factor = jnp.where(row_owner[:, None, None] == column_owner[None, :, :], 4.0, 1.0)
    return mixed_field * row_scale[:, None, None] * col_scale[None, :, :] * spike_factor


def centred(stream_key, shape, width, reach, dtype=jnp.bfloat16):
    result = width * jax.random.normal(stream_key, shape, jnp.float32)
    return jnp.clip(result, min=-reach, max=reach).astype(dtype)


def setup_inputs(seed: int = 0) -> dict:
    keys = jax.random.split(jax.random.key(seed), 3)
    tensor_slab = draw_tensor_slab(jax.random.fold_in(keys[2], 71), 0)
    start_matrix = centred(keys[1], (MODE, RANK), 1.0, 6.0, jnp.float32)
    return dict(tensor_slab=tensor_slab, start_matrix=start_matrix)


HIGHEST = lax.Precision.HIGHEST

def orthonormal(projected):
    small_gram = jnp.dot(projected.T.astype(jnp.float32), projected.astype(jnp.float32), precision=HIGHEST, preferred_element_type=jnp.float32)
    factor = jnp.linalg.cholesky(small_gram)
    return lax.linalg.triangular_solve(factor, projected, left_side=False, lower=True, transpose_a=True)

def reference(tensor_slab, start_matrix):
    columns = tensor_slab.reshape(MODE, SLICES * CELLS)
    gram_matrix = jnp.dot(columns.astype(jnp.float32), columns.T.astype(jnp.float32), precision=HIGHEST, preferred_element_type=jnp.float32) * (1.0 / (SLICES * CELLS))
    triangle = jnp.linalg.cholesky(gram_matrix)
    subspace_basis = start_matrix
    for iteration in range(ITERS):
        inner_part = jnp.dot(triangle.T.astype(jnp.float32), subspace_basis.astype(jnp.float32), precision=HIGHEST, preferred_element_type=jnp.float32)
        projected = jnp.dot(triangle.astype(jnp.float32), inner_part.astype(jnp.float32), precision=HIGHEST, preferred_element_type=jnp.float32)
        subspace_basis = orthonormal(projected)
    core_tensor = jnp.dot(subspace_basis.T.astype(jnp.float32), columns.astype(jnp.float32), precision=HIGHEST, preferred_element_type=jnp.float32)
    return (triangle, subspace_basis, core_tensor.reshape(RANK, SLICES, CELLS))
```

```python
import functools

import jax
import jax.numpy as jnp
from jax import lax
from jax.experimental import pallas as pl
from jax.experimental.pallas import tpu as pltpu
from jax.sharding import PartitionSpec as P

ITERS = 2
HIGHEST = lax.Precision.HIGHEST
BLOCK = 128
MESH = pl.DeviceIdType.MESH


def product(left_side, right_side):
    return jnp.dot(left_side, right_side, precision=HIGHEST, preferred_element_type=jnp.float32)


def dot_nt(a, b):
    return lax.dot_general(a, b, (((1,), (1,)), ((), ())), preferred_element_type=jnp.float32)


def split_two(value):
    high = value.astype(jnp.bfloat16)
    low = (value - high.astype(jnp.float32)).astype(jnp.bfloat16)
    return high, low


def exchange_kernel(
    nf, ng, chunks, per_slice, slices, width, rows, piece, scale,
    x_ref, high_ref, low_ref, gram_ref,
    xbuf, acc, packed, group_in, group_sum, fiber_in,
    own_sem, a_send, a_recv, g_send, g_recv, f_send, f_recv, fa_send, fa_recv, ga_send, ga_recv,
):
    mf = lax.axis_index("fiber")
    mg = lax.axis_index("group")
    barrier = pltpu.get_barrier_semaphore()
    for k in range(1, nf):
        pl.semaphore_signal(barrier, inc=1, device_id=(lax.rem(mf + k, nf), mg), device_id_type=MESH)
    for k in range(1, ng):
        pl.semaphore_signal(barrier, inc=1, device_id=(mf, lax.rem(mg + k, ng)), device_id_type=MESH)
    pl.semaphore_wait(barrier, nf + ng - 2)

    def slab_copy(c, k):
        peer = lax.rem(mf + k, nf)
        s, h = c // per_slice, c % per_slice
        return pltpu.make_async_remote_copy(
            src_ref=x_ref.at[peer * slices + s, :, pl.ds(pl.multiple_of(h * width, width), width)],
            dst_ref=xbuf.at[c, pl.ds(pl.multiple_of(mf * rows, rows), rows), :],
            send_sem=a_send.at[k - 1, c],
            recv_sem=a_recv.at[k - 1, c],
            device_id=(peer, mg),
            device_id_type=MESH,
        )

    def own_copy(c):
        s, h = c // per_slice, c % per_slice
        return pltpu.make_async_copy(
            x_ref.at[mf * slices + s, :, pl.ds(pl.multiple_of(h * width, width), width)],
            xbuf.at[c, pl.ds(pl.multiple_of(mf * rows, rows), rows), :],
            own_sem.at[c],
        )

    def start_chunk(c, _):
        for k in range(1, nf):
            slab_copy(c, k).start()
        own_copy(c).start()
        return 0

    lax.fori_loop(0, chunks, start_chunk, 0)
    acc[...] = jnp.zeros_like(acc)

    def use_chunk(c, _):
        own_copy(c).wait()
        for k in range(1, nf):
            slab_copy(c, k).wait_recv()
        high, low = split_two(xbuf[c])
        high_ref[c] = high
        low_ref[c] = low
        acc[...] += dot_nt(high, high) + (dot_nt(high, low) + dot_nt(low, high))
        return 0

    lax.fori_loop(0, chunks, use_chunk, 0)

    blocks = acc.shape[0] // BLOCK
    at = 0
    for i in range(blocks):
        for j in range(i + 1):
            packed[at * BLOCK:(at + 1) * BLOCK, :] = (
                acc[i * BLOCK:(i + 1) * BLOCK, j * BLOCK:(j + 1) * BLOCK] * scale
            )
            at += 1
    if at * BLOCK < packed.shape[0]:
        packed[at * BLOCK:, :] = jnp.zeros((packed.shape[0] - at * BLOCK, BLOCK), jnp.float32)

    big = piece * nf

    def group_copy(k):
        peer = lax.rem(mg + k, ng)
        return pltpu.make_async_remote_copy(
            src_ref=packed.at[pl.ds(pl.multiple_of(peer * big, 8), big), :],
            dst_ref=group_in.at[k - 1],
            send_sem=g_send.at[k - 1],
            recv_sem=g_recv.at[k - 1],
            device_id=(mf, peer),
            device_id_type=MESH,
        )

    for k in range(1, ng):
        group_copy(k).start()
    group_sum[...] = packed[pl.ds(pl.multiple_of(mg * big, 8), big), :]
    for k in range(1, ng):
        group_copy(k).wait_recv()
        group_sum[...] += group_in[k - 1]

    def fiber_copy(k):
        peer = lax.rem(mf + k, nf)
        return pltpu.make_async_remote_copy(
            src_ref=group_sum.at[pl.ds(pl.multiple_of(peer * piece, 8), piece), :],
            dst_ref=fiber_in.at[k - 1],
            send_sem=f_send.at[k - 1],
            recv_sem=f_recv.at[k - 1],
            device_id=(peer, mg),
            device_id_type=MESH,
        )

    for k in range(1, nf):
        fiber_copy(k).start()
    total = group_sum[pl.ds(pl.multiple_of(mf * piece, 8), piece), :]
    for k in range(1, nf):
        fiber_copy(k).wait_recv()
        total += fiber_in[k - 1]
    mine = pl.ds(pl.multiple_of(mg * big + mf * piece, 8), piece)
    gram_ref[mine, :] = total

    def fiber_gather(k):
        return pltpu.make_async_remote_copy(
            src_ref=gram_ref.at[mine, :],
            dst_ref=gram_ref.at[mine, :],
            send_sem=fa_send.at[k - 1],
            recv_sem=fa_recv.at[k - 1],
            device_id=(lax.rem(mf + k, nf), mg),
            device_id_type=MESH,
        )

    for k in range(1, nf):
        fiber_gather(k).start()
    for k in range(1, nf):
        fiber_gather(k).wait_recv()

    def group_gather(k):
        part = pl.ds(pl.multiple_of(mg * big, 8), big)
        return pltpu.make_async_remote_copy(
            src_ref=gram_ref.at[part, :],
            dst_ref=gram_ref.at[part, :],
            send_sem=ga_send.at[k - 1],
            recv_sem=ga_recv.at[k - 1],
            device_id=(mf, lax.rem(mg + k, ng)),
            device_id_type=MESH,
        )

    for k in range(1, ng):
        group_gather(k).start()
    for k in range(1, ng):
        group_gather(k).wait_recv()

    def end_chunk(c, _):
        for k in range(1, nf):
            slab_copy(c, k).wait_send()
        return 0

    lax.fori_loop(0, chunks, end_chunk, 0)
    for k in range(1, ng):
        group_copy(k).wait_send()
        group_gather(k).wait_send()
    for k in range(1, nf):
        fiber_copy(k).wait_send()
        fiber_gather(k).wait_send()


def exchange_and_gram(tensor_slab, nf, ng):
    rows, all_slices, cells = tensor_slab.shape
    slices = all_slices // nf
    modes = rows * nf
    width = 512 if cells % 512 == 0 else cells
    per_slice = cells // width
    chunks = slices * per_slice
    blocks = modes // BLOCK
    packed_rows = blocks * (blocks + 1) // 2 * BLOCK
    piece = -(-packed_rows // (nf * ng * 8)) * 8
    total_rows = piece * nf * ng
    scale = 1.0 / (all_slices * cells * ng)
    x = jnp.transpose(tensor_slab, (1, 0, 2))
    kernel = functools.partial(
        exchange_kernel, nf, ng, chunks, per_slice, slices, width, rows, piece, scale
    )
    dma = pltpu.SemaphoreType.DMA
    vmem = pl.BlockSpec(memory_space=pltpu.VMEM)
    high, low, gram = pl.pallas_call(
        kernel,
        out_shape=(
            jax.ShapeDtypeStruct((chunks, modes, width), jnp.bfloat16),
            jax.ShapeDtypeStruct((chunks, modes, width), jnp.bfloat16),
            jax.ShapeDtypeStruct((total_rows, BLOCK), jnp.float32),
        ),
        in_specs=[pl.BlockSpec(memory_space=pl.ANY)],
        out_specs=(vmem, vmem, vmem),
        scratch_shapes=[
            pltpu.VMEM((chunks, modes, width), jnp.float32),
            pltpu.VMEM((modes, modes), jnp.float32),
            pltpu.VMEM((total_rows, BLOCK), jnp.float32),
            pltpu.VMEM((ng - 1, piece * nf, BLOCK), jnp.float32),
            pltpu.VMEM((piece * nf, BLOCK), jnp.float32),
            pltpu.VMEM((nf - 1, piece, BLOCK), jnp.float32),
            dma((chunks,)),
            dma((nf - 1, chunks)),
            dma((nf - 1, chunks)),
            dma((ng - 1,)),
            dma((ng - 1,)),
            dma((nf - 1,)),
            dma((nf - 1,)),
            dma((nf - 1,)),
            dma((nf - 1,)),
            dma((ng - 1,)),
            dma((ng - 1,)),
        ],
        compiler_params=pltpu.CompilerParams(
            collective_id=0, has_side_effects=True, vmem_limit_bytes=56 * 1024 * 1024
        ),
    )(x)
    full = [[None] * blocks for _ in range(blocks)]
    at = 0
    for i in range(blocks):
        for j in range(i + 1):
            full[i][j] = gram[at * BLOCK:(at + 1) * BLOCK]
            if j < i:
                full[j][i] = full[i][j].T
            at += 1
    return high, low, jnp.block(full)


def project_kernel(per_slice, basis_ref, high_ref, low_ref, out_ref):
    b_high, b_low = split_two(basis_ref[...].T)
    width = high_ref.shape[2]

    def step(c, _):
        s, h = c // per_slice, c % per_slice
        high, low = high_ref[c], low_ref[c]
        value = jnp.dot(b_high, high, preferred_element_type=jnp.float32)
        value += jnp.dot(b_high, low, preferred_element_type=jnp.float32)
        value += jnp.dot(b_low, high, preferred_element_type=jnp.float32)
        out_ref[s, :, pl.ds(pl.multiple_of(h * width, width), width)] = value
        return 0

    lax.fori_loop(0, high_ref.shape[0], step, 0)


def project(basis, high, low, slices, cells):
    per_slice = cells // high.shape[2]
    vmem = pl.BlockSpec(memory_space=pltpu.VMEM)
    core = pl.pallas_call(
        functools.partial(project_kernel, per_slice),
        out_shape=jax.ShapeDtypeStruct((slices, basis.shape[1], cells), jnp.float32),
        in_specs=[vmem, vmem, vmem],
        out_specs=vmem,
        compiler_params=pltpu.CompilerParams(vmem_limit_bytes=56 * 1024 * 1024),
    )(basis, high, low)
    return jnp.transpose(core, (1, 0, 2))


def orthonormal(projected):
    small_gram = product(projected.T, projected)
    factor = jnp.linalg.cholesky(small_gram)
    return lax.linalg.triangular_solve(
        factor, projected, left_side=False, lower=True, transpose_a=True
    )


def shards(nf, ng, tensor_slab, start_matrix):
    high, low, gram = exchange_and_gram(tensor_slab, nf, ng)
    triangle = jnp.linalg.cholesky(gram)
    subspace_basis = start_matrix
    for iteration in range(ITERS):
        subspace_basis = orthonormal(product(gram, subspace_basis))
    core_tensor = project(
        subspace_basis, high, low, tensor_slab.shape[1] // nf, tensor_slab.shape[2]
    )
    return (triangle, subspace_basis, core_tensor)


def solution(mesh):
    placed = (P("fiber", None, "group"), P())
    return jax.shard_map(
        functools.partial(shards, mesh.shape["fiber"], mesh.shape["group"]),
        mesh=mesh,
        in_specs=placed,
        out_specs=(P(), P(), P(None, "fiber", "group")),
        check_vma=False,
    )
```

```python
import functools

import jax
import jax.numpy as jnp
from jax import lax
from jax.experimental import pallas as pl
from jax.experimental.pallas import tpu as pltpu
from jax.sharding import PartitionSpec as P

ITERS = 2
HIGHEST = lax.Precision.HIGHEST
BLOCK = 128
MESH = pl.DeviceIdType.MESH


def product(left_side, right_side):
    return jnp.dot(left_side, right_side, precision=HIGHEST, preferred_element_type=jnp.float32)


def dot_nt(a, b):
    return lax.dot_general(a, b, (((1,), (1,)), ((), ())), preferred_element_type=jnp.float32)


def split_two(value):
    high = value.astype(jnp.bfloat16)
    low = (value - high.astype(jnp.float32)).astype(jnp.bfloat16)
    return high, low


def exchange_kernel(
    nf, ng, chunks, per_slice, slices, width, rows, piece, scale,
    x_ref, high_ref, low_ref, gram_ref,
    xbuf, acc, packed, group_in, group_sum, fiber_in,
    own_sem, a_send, a_recv, g_send, g_recv, f_send, f_recv, fa_send, fa_recv, ga_send, ga_recv,
):
    mf = lax.axis_index("fiber")
    mg = lax.axis_index("group")
    barrier = pltpu.get_barrier_semaphore()
    for k in range(1, nf):
        pl.semaphore_signal(barrier, inc=1, device_id=(lax.rem(mf + k, nf), mg), device_id_type=MESH)
    for k in range(1, ng):
        pl.semaphore_signal(barrier, inc=1, device_id=(mf, lax.rem(mg + k, ng)), device_id_type=MESH)
    pl.semaphore_wait(barrier, nf + ng - 2)

    def slab_copy(c, k):
        peer = lax.rem(mf + k, nf)
        s, h = c // per_slice, c % per_slice
        return pltpu.make_async_remote_copy(
            src_ref=x_ref.at[peer * slices + s, :, pl.ds(pl.multiple_of(h * width, width), width)],
            dst_ref=xbuf.at[c, pl.ds(pl.multiple_of(mf * rows, rows), rows), :],
            send_sem=a_send.at[k - 1, c],
            recv_sem=a_recv.at[k - 1, c],
            device_id=(peer, mg),
            device_id_type=MESH,
        )

    def own_copy(c):
        s, h = c // per_slice, c % per_slice
        return pltpu.make_async_copy(
            x_ref.at[mf * slices + s, :, pl.ds(pl.multiple_of(h * width, width), width)],
            xbuf.at[c, pl.ds(pl.multiple_of(mf * rows, rows), rows), :],
            own_sem.at[c],
        )

    def start_chunk(c, _):
        for k in range(1, nf):
            slab_copy(c, k).start()
        own_copy(c).start()
        return 0

    lax.fori_loop(0, chunks, start_chunk, 0)
    acc[...] = jnp.zeros_like(acc)

    def use_chunk(c, _):
        own_copy(c).wait()
        for k in range(1, nf):
            slab_copy(c, k).wait_recv()
        high, low = split_two(xbuf[c])
        high_ref[c] = high
        low_ref[c] = low
        acc[...] += dot_nt(high, high) + (dot_nt(high, low) + dot_nt(low, high))
        return 0

    lax.fori_loop(0, chunks, use_chunk, 0)

    blocks = acc.shape[0] // BLOCK
    at = 0
    for i in range(blocks):
        for j in range(i + 1):
            packed[at * BLOCK:(at + 1) * BLOCK, :] = (
                acc[i * BLOCK:(i + 1) * BLOCK, j * BLOCK:(j + 1) * BLOCK] * scale
            )
            at += 1
    if at * BLOCK < packed.shape[0]:
        packed[at * BLOCK:, :] = jnp.zeros((packed.shape[0] - at * BLOCK, BLOCK), jnp.float32)

    big = piece * nf

    def group_copy(k):
        peer = lax.rem(mg + k, ng)
        return pltpu.make_async_remote_copy(
            src_ref=packed.at[pl.ds(pl.multiple_of(peer * big, 8), big), :],
            dst_ref=group_in.at[k - 1],
            send_sem=g_send.at[k - 1],
            recv_sem=g_recv.at[k - 1],
            device_id=(mf, peer),
            device_id_type=MESH,
        )

    for k in range(1, ng):
        group_copy(k).start()
    group_sum[...] = packed[pl.ds(pl.multiple_of(mg * big, 8), big), :]
    for k in range(1, ng):
        group_copy(k).wait_recv()
        group_sum[...] += group_in[k - 1]

    def fiber_copy(k):
        peer = lax.rem(mf + k, nf)
        return pltpu.make_async_remote_copy(
            src_ref=group_sum.at[pl.ds(pl.multiple_of(peer * piece, 8), piece), :],
            dst_ref=fiber_in.at[k - 1],
            send_sem=f_send.at[k - 1],
            recv_sem=f_recv.at[k - 1],
            device_id=(peer, mg),
            device_id_type=MESH,
        )

    for k in range(1, nf):
        fiber_copy(k).start()
    total = group_sum[pl.ds(pl.multiple_of(mf * piece, 8), piece), :]
    for k in range(1, nf):
        fiber_copy(k).wait_recv()
        total += fiber_in[k - 1]
    mine = pl.ds(pl.multiple_of(mg * big + mf * piece, 8), piece)
    gram_ref[mine, :] = total

    def fiber_gather(k):
        return pltpu.make_async_remote_copy(
            src_ref=gram_ref.at[mine, :],
            dst_ref=gram_ref.at[mine, :],
            send_sem=fa_send.at[k - 1],
            recv_sem=fa_recv.at[k - 1],
            device_id=(lax.rem(mf + k, nf), mg),
            device_id_type=MESH,
        )

    for k in range(1, nf):
        fiber_gather(k).start()
    for k in range(1, nf):
        fiber_gather(k).wait_recv()

    def group_gather(k):
        part = pl.ds(pl.multiple_of(mg * big, 8), big)
        return pltpu.make_async_remote_copy(
            src_ref=gram_ref.at[part, :],
            dst_ref=gram_ref.at[part, :],
            send_sem=ga_send.at[k - 1],
            recv_sem=ga_recv.at[k - 1],
            device_id=(mf, lax.rem(mg + k, ng)),
            device_id_type=MESH,
        )

    for k in range(1, ng):
        group_gather(k).start()
    for k in range(1, ng):
        group_gather(k).wait_recv()

    def end_chunk(c, _):
        for k in range(1, nf):
            slab_copy(c, k).wait_send()
        return 0

    lax.fori_loop(0, chunks, end_chunk, 0)
    for k in range(1, ng):
        group_copy(k).wait_send()
        group_gather(k).wait_send()
    for k in range(1, nf):
        fiber_copy(k).wait_send()
        fiber_gather(k).wait_send()


def exchange_and_gram(tensor_slab, nf, ng):
    rows, all_slices, cells = tensor_slab.shape
    slices = all_slices // nf
    modes = rows * nf
    width = 512 if cells % 512 == 0 else cells
    per_slice = cells // width
    chunks = slices * per_slice
    blocks = modes // BLOCK
    packed_rows = blocks * (blocks + 1) // 2 * BLOCK
    piece = -(-packed_rows // (nf * ng * 8)) * 8
    total_rows = piece * nf * ng
    scale = 1.0 / (all_slices * cells * ng)
    x = jnp.transpose(tensor_slab, (1, 0, 2))
    kernel = functools.partial(
        exchange_kernel, nf, ng, chunks, per_slice, slices, width, rows, piece, scale
    )
    dma = pltpu.SemaphoreType.DMA
    vmem = pl.BlockSpec(memory_space=pltpu.VMEM)
    high, low, gram = pl.pallas_call(
        kernel,
        out_shape=(
            jax.ShapeDtypeStruct((chunks, modes, width), jnp.bfloat16),
            jax.ShapeDtypeStruct((chunks, modes, width), jnp.bfloat16),
            jax.ShapeDtypeStruct((total_rows, BLOCK), jnp.float32),
        ),
        in_specs=[pl.BlockSpec(memory_space=pl.ANY)],
        out_specs=(vmem, vmem, vmem),
        scratch_shapes=[
            pltpu.VMEM((chunks, modes, width), jnp.float32),
            pltpu.VMEM((modes, modes), jnp.float32),
            pltpu.VMEM((total_rows, BLOCK), jnp.float32),
            pltpu.VMEM((ng - 1, piece * nf, BLOCK), jnp.float32),
            pltpu.VMEM((piece * nf, BLOCK), jnp.float32),
            pltpu.VMEM((nf - 1, piece, BLOCK), jnp.float32),
            dma((chunks,)),
            dma((nf - 1, chunks)),
            dma((nf - 1, chunks)),
            dma((ng - 1,)),
            dma((ng - 1,)),
            dma((nf - 1,)),
            dma((nf - 1,)),
            dma((nf - 1,)),
            dma((nf - 1,)),
            dma((ng - 1,)),
            dma((ng - 1,)),
        ],
        compiler_params=pltpu.CompilerParams(
            collective_id=0, has_side_effects=True, vmem_limit_bytes=56 * 1024 * 1024
        ),
    )(x)
    full = [[None] * blocks for _ in range(blocks)]
    at = 0
    for i in range(blocks):
        for j in range(i + 1):
            full[i][j] = gram[at * BLOCK:(at + 1) * BLOCK]
            if j < i:
                full[j][i] = full[i][j].T
            at += 1
    return high, low, jnp.block(full)


def dot_tn(a, b):
    return lax.dot_general(
        a, b, (((0,), (0,)), ((), ())), precision=HIGHEST, preferred_element_type=jnp.float32
    )


def product_nt(a, b):
    return lax.dot_general(
        a, b, (((1,), (1,)), ((), ())), precision=HIGHEST, preferred_element_type=jnp.float32
    )


def factor_many(matrices):
    n = BLOCK
    row = lax.broadcasted_iota(jnp.int32, (n, n), 0)
    col = lax.broadcasted_iota(jnp.int32, (n, n), 1)
    eye = jnp.where(row == col, 1.0, 0.0).astype(jnp.float32)
    rest = [jnp.concatenate([m, eye], axis=1) for m in matrices]
    done = [[] for _ in matrices]
    for k in range(n // 8):
        panels = [w[:8] for w in rest]
        corners = [
            [jnp.broadcast_to(p[:, 8 * k + t:8 * k + t + 1], (8, n)) for t in range(8)]
            for p in panels
        ]
        rows = [[] for _ in matrices]
        for t in range(8):
            for q in range(len(matrices)):
                pivot = corners[q][t][t:t + 1]
                inverse = lax.rsqrt(pivot)
                c = corners[q][t] * inverse
                for v in range(t + 1, 8):
                    corners[q][v] = corners[q][v] - c * c[v:v + 1]
                wide = jnp.concatenate([inverse, inverse], axis=1)
                r = panels[q][t:t + 1] * wide
                rows[q].append(r)
                panels[q] = panels[q] - jnp.concatenate([c, c], axis=1) * r
        for q in range(len(matrices)):
            panel = jnp.concatenate(rows[q], axis=0)
            done[q].append(panel)
            if 8 * (k + 1) < n:
                update = dot_tn(panel[:, :n], panel)
                rest[q] = rest[q][8:] - update[8 * (k + 1):]
    result = []
    for q in range(len(matrices)):
        both = jnp.concatenate(done[q], axis=0)
        lower = jnp.where(row >= col, both[:, :n].T, 0.0)
        result.append((lower, both[:, n:]))
    return result


def factor_kernel(per_slice, start_ref, gram_ref, high_ref, low_ref, tri_ref, basis_ref, core_ref, work):
    modes = gram_ref.shape[0]
    blocks = modes // BLOCK
    work[...] = gram_ref[...]
    tri_ref[...] = jnp.zeros_like(tri_ref)
    basis = start_ref[...].T

    def projected_gram(basis):
        projected = product(basis, gram_ref[...])
        return projected, product_nt(projected, projected)

    projected, small = projected_gram(basis)
    for i in range(max(blocks, ITERS)):
        matrices = []
        if i < blocks:
            lo = i * BLOCK
            matrices.append(work[lo:lo + BLOCK, lo:lo + BLOCK])
        if i < ITERS:
            matrices.append(small)
        factors = factor_many(matrices)
        if i < ITERS:
            basis = product(factors[-1][1], projected)
            if i + 1 < ITERS:
                projected, small = projected_gram(basis)
            else:
                basis_ref[...] = basis.T
        if i < blocks:
            lower, inverse = factors[0]
            tri_ref[lo:lo + BLOCK, lo:lo + BLOCK] = lower
            if i + 1 < blocks:
                below = product_nt(work[lo + BLOCK:, lo:lo + BLOCK], inverse)
                tri_ref[lo + BLOCK:, lo:lo + BLOCK] = below
                work[lo + BLOCK:, lo + BLOCK:] = work[lo + BLOCK:, lo + BLOCK:] - product_nt(below, below)

    b_high, b_low = split_two(basis)
    width = high_ref.shape[2]

    def step(c, _):
        s, h = c // per_slice, c % per_slice
        high, low = high_ref[c], low_ref[c]
        value = jnp.dot(b_high, high, preferred_element_type=jnp.float32)
        value += jnp.dot(b_high, low, preferred_element_type=jnp.float32)
        value += jnp.dot(b_low, high, preferred_element_type=jnp.float32)
        core_ref[s, :, pl.ds(pl.multiple_of(h * width, width), width)] = value
        return 0

    lax.fori_loop(0, high_ref.shape[0], step, 0)


def shards(nf, ng, tensor_slab, start_matrix):
    high, low, gram = exchange_and_gram(tensor_slab, nf, ng)
    slices, cells = tensor_slab.shape[1] // nf, tensor_slab.shape[2]
    modes, rank = start_matrix.shape
    vmem = pl.BlockSpec(memory_space=pltpu.VMEM)
    triangle, basis, core = pl.pallas_call(
        functools.partial(factor_kernel, cells // high.shape[2]),
        out_shape=(
            jax.ShapeDtypeStruct((modes, modes), jnp.float32),
            jax.ShapeDtypeStruct((modes, rank), jnp.float32),
            jax.ShapeDtypeStruct((slices, rank, cells), jnp.float32),
        ),
        in_specs=[vmem] * 4,
        out_specs=(vmem, vmem, vmem),
        scratch_shapes=[pltpu.VMEM((modes, modes), jnp.float32)],
        compiler_params=pltpu.CompilerParams(vmem_limit_bytes=56 * 1024 * 1024),
    )(start_matrix, gram, high, low)
    return (triangle, basis, jnp.transpose(core, (1, 0, 2)))


def solution(mesh):
    placed = (P("fiber", None, "group"), P())
    return jax.shard_map(
        functools.partial(shards, mesh.shape["fiber"], mesh.shape["group"]),
        mesh=mesh,
        in_specs=placed,
        out_specs=(P(), P(), P(None, "fiber", "group")),
        check_vma=False,
    )
```

```python
import functools

import jax
import jax.numpy as jnp
from jax import lax
from jax.experimental import pallas as pl
from jax.experimental.pallas import tpu as pltpu
from jax.sharding import PartitionSpec as P

ITERS = 2
HIGHEST = lax.Precision.HIGHEST
BLOCK = 128
MESH = pl.DeviceIdType.MESH


def product(left_side, right_side):
    return jnp.dot(left_side, right_side, precision=HIGHEST, preferred_element_type=jnp.float32)


def dot_nt(a, b):
    return lax.dot_general(a, b, (((1,), (1,)), ((), ())), preferred_element_type=jnp.float32)


def split_two(value):
    high = value.astype(jnp.bfloat16)
    low = (value - high.astype(jnp.float32)).astype(jnp.bfloat16)
    return high, low


def exchange_kernel(
    nf, ng, chunks, per_slice, slices, width, rows, piece, scale,
    x_ref, high_ref, low_ref, gram_ref,
    xbuf, acc, packed, group_in, group_sum, fiber_in,
    own_sem, a_send, a_recv, g_send, g_recv, f_send, f_recv, fa_send, fa_recv, ga_send, ga_recv,
):
    mf = lax.axis_index("fiber")
    mg = lax.axis_index("group")
    barrier = pltpu.get_barrier_semaphore()
    for k in range(1, nf):
        pl.semaphore_signal(barrier, inc=1, device_id=(lax.rem(mf + k, nf), mg), device_id_type=MESH)
    for k in range(1, ng):
        pl.semaphore_signal(barrier, inc=1, device_id=(mf, lax.rem(mg + k, ng)), device_id_type=MESH)
    pl.semaphore_wait(barrier, nf + ng - 2)

    def slab_copy(c, k):
        peer = lax.rem(mf + k, nf)
        s, h = c // per_slice, c % per_slice
        return pltpu.make_async_remote_copy(
            src_ref=x_ref.at[:, peer * slices + s, pl.ds(pl.multiple_of(h * width, width), width)],
            dst_ref=xbuf.at[c, pl.ds(pl.multiple_of(mf * rows, rows), rows), :],
            send_sem=a_send.at[k - 1, c],
            recv_sem=a_recv.at[k - 1, c],
            device_id=(peer, mg),
            device_id_type=MESH,
        )

    def own_copy(c):
        s, h = c // per_slice, c % per_slice
        return pltpu.make_async_copy(
            x_ref.at[:, mf * slices + s, pl.ds(pl.multiple_of(h * width, width), width)],
            xbuf.at[c, pl.ds(pl.multiple_of(mf * rows, rows), rows), :],
            own_sem.at[c],
        )

    def start_chunk(c, _):
        for k in range(1, nf):
            slab_copy(c, k).start()
        own_copy(c).start()
        return 0

    lax.fori_loop(0, chunks, start_chunk, 0)
    acc[...] = jnp.zeros_like(acc)

    def use_chunk(c, _):
        own_copy(c).wait()
        for k in range(1, nf):
            slab_copy(c, k).wait_recv()
        high, low = split_two(xbuf[c])
        high_ref[c] = high
        low_ref[c] = low
        acc[...] += dot_nt(high, high) + (dot_nt(high, low) + dot_nt(low, high))
        return 0

    lax.fori_loop(0, chunks, use_chunk, 0)

    blocks = acc.shape[0] // BLOCK
    at = 0
    for i in range(blocks):
        for j in range(i + 1):
            packed[at * BLOCK:(at + 1) * BLOCK, :] = (
                acc[i * BLOCK:(i + 1) * BLOCK, j * BLOCK:(j + 1) * BLOCK] * scale
            )
            at += 1
    if at * BLOCK < packed.shape[0]:
        packed[at * BLOCK:, :] = jnp.zeros((packed.shape[0] - at * BLOCK, BLOCK), jnp.float32)

    big = piece * nf

    def group_copy(k):
        peer = lax.rem(mg + k, ng)
        return pltpu.make_async_remote_copy(
            src_ref=packed.at[pl.ds(pl.multiple_of(peer * big, 8), big), :],
            dst_ref=group_in.at[k - 1],
            send_sem=g_send.at[k - 1],
            recv_sem=g_recv.at[k - 1],
            device_id=(mf, peer),
            device_id_type=MESH,
        )

    for k in range(1, ng):
        group_copy(k).start()
    group_sum[...] = packed[pl.ds(pl.multiple_of(mg * big, 8), big), :]
    for k in range(1, ng):
        group_copy(k).wait_recv()
        group_sum[...] += group_in[k - 1]

    def fiber_copy(k):
        peer = lax.rem(mf + k, nf)
        return pltpu.make_async_remote_copy(
            src_ref=group_sum.at[pl.ds(pl.multiple_of(peer * piece, 8), piece), :],
            dst_ref=fiber_in.at[k - 1],
            send_sem=f_send.at[k - 1],
            recv_sem=f_recv.at[k - 1],
            device_id=(peer, mg),
            device_id_type=MESH,
        )

    for k in range(1, nf):
        fiber_copy(k).start()
    total = group_sum[pl.ds(pl.multiple_of(mf * piece, 8), piece), :]
    for k in range(1, nf):
        fiber_copy(k).wait_recv()
        total += fiber_in[k - 1]
    mine = pl.ds(pl.multiple_of(mg * big + mf * piece, 8), piece)
    gram_ref[mine, :] = total

    def fiber_gather(k):
        return pltpu.make_async_remote_copy(
            src_ref=gram_ref.at[mine, :],
            dst_ref=gram_ref.at[mine, :],
            send_sem=fa_send.at[k - 1],
            recv_sem=fa_recv.at[k - 1],
            device_id=(lax.rem(mf + k, nf), mg),
            device_id_type=MESH,
        )

    for k in range(1, nf):
        fiber_gather(k).start()
    for k in range(1, nf):
        fiber_gather(k).wait_recv()

    def group_gather(k):
        part = pl.ds(pl.multiple_of(mg * big, 8), big)
        return pltpu.make_async_remote_copy(
            src_ref=gram_ref.at[part, :],
            dst_ref=gram_ref.at[part, :],
            send_sem=ga_send.at[k - 1],
            recv_sem=ga_recv.at[k - 1],
            device_id=(mf, lax.rem(mg + k, ng)),
            device_id_type=MESH,
        )

    for k in range(1, ng):
        group_gather(k).start()
    for k in range(1, ng):
        group_gather(k).wait_recv()

    def end_chunk(c, _):
        for k in range(1, nf):
            slab_copy(c, k).wait_send()
        return 0

    lax.fori_loop(0, chunks, end_chunk, 0)
    for k in range(1, ng):
        group_copy(k).wait_send()
        group_gather(k).wait_send()
    for k in range(1, nf):
        fiber_copy(k).wait_send()
        fiber_gather(k).wait_send()


def exchange_and_gram(tensor_slab, nf, ng):
    rows, all_slices, cells = tensor_slab.shape
    slices = all_slices // nf
    modes = rows * nf
    width = 512 if cells % 512 == 0 else cells
    per_slice = cells // width
    chunks = slices * per_slice
    blocks = modes // BLOCK
    packed_rows = blocks * (blocks + 1) // 2 * BLOCK
    piece = -(-packed_rows // (nf * ng * 8)) * 8
    total_rows = piece * nf * ng
    scale = 1.0 / (all_slices * cells * ng)
    kernel = functools.partial(
        exchange_kernel, nf, ng, chunks, per_slice, slices, width, rows, piece, scale
    )
    dma = pltpu.SemaphoreType.DMA
    vmem = pl.BlockSpec(memory_space=pltpu.VMEM)
    high, low, gram = pl.pallas_call(
        kernel,
        out_shape=(
            jax.ShapeDtypeStruct((chunks, modes, width), jnp.bfloat16),
            jax.ShapeDtypeStruct((chunks, modes, width), jnp.bfloat16),
            jax.ShapeDtypeStruct((total_rows, BLOCK), jnp.float32),
        ),
        in_specs=[pl.BlockSpec(memory_space=pl.ANY)],
        out_specs=(vmem, vmem, vmem),
        scratch_shapes=[
            pltpu.VMEM((chunks, modes, width), jnp.float32),
            pltpu.VMEM((modes, modes), jnp.float32),
            pltpu.VMEM((total_rows, BLOCK), jnp.float32),
            pltpu.VMEM((ng - 1, piece * nf, BLOCK), jnp.float32),
            pltpu.VMEM((piece * nf, BLOCK), jnp.float32),
            pltpu.VMEM((nf - 1, piece, BLOCK), jnp.float32),
            dma((chunks,)),
            dma((nf - 1, chunks)),
            dma((nf - 1, chunks)),
            dma((ng - 1,)),
            dma((ng - 1,)),
            dma((nf - 1,)),
            dma((nf - 1,)),
            dma((nf - 1,)),
            dma((nf - 1,)),
            dma((ng - 1,)),
            dma((ng - 1,)),
        ],
        compiler_params=pltpu.CompilerParams(
            collective_id=0, has_side_effects=True, vmem_limit_bytes=56 * 1024 * 1024
        ),
    )(tensor_slab)
    return high, low, gram


def dot_tn(a, b):
    return lax.dot_general(
        a, b, (((0,), (0,)), ((), ())), precision=HIGHEST, preferred_element_type=jnp.float32
    )


def product_nt(a, b):
    return lax.dot_general(
        a, b, (((1,), (1,)), ((), ())), precision=HIGHEST, preferred_element_type=jnp.float32
    )


def factor_many(matrices):
    n = BLOCK
    row = lax.broadcasted_iota(jnp.int32, (n, n), 0)
    col = lax.broadcasted_iota(jnp.int32, (n, n), 1)
    eye = jnp.where(row == col, 1.0, 0.0).astype(jnp.float32)
    rest = [jnp.concatenate([m, eye], axis=1) for m in matrices]
    done = [[] for _ in matrices]
    for k in range(n // 8):
        panels = [w[:8] for w in rest]
        corners = [
            [jnp.broadcast_to(p[:, 8 * k + t:8 * k + t + 1], (8, n)) for t in range(8)]
            for p in panels
        ]
        rows = [[] for _ in matrices]
        for t in range(8):
            for q in range(len(matrices)):
                pivot = corners[q][t][t:t + 1]
                inverse = lax.rsqrt(pivot)
                c = corners[q][t] * inverse
                for v in range(t + 1, 8):
                    corners[q][v] = corners[q][v] - c * c[v:v + 1]
                wide = jnp.concatenate([inverse, inverse], axis=1)
                r = panels[q][t:t + 1] * wide
                rows[q].append(r)
                panels[q] = panels[q] - jnp.concatenate([c, c], axis=1) * r
        for q in range(len(matrices)):
            panel = jnp.concatenate(rows[q], axis=0)
            done[q].append(panel)
            if 8 * (k + 1) < n:
                update = dot_tn(panel[:, :n], panel)
                rest[q] = rest[q][8:] - update[8 * (k + 1):]
    result = []
    for q in range(len(matrices)):
        both = jnp.concatenate(done[q], axis=0)
        lower = jnp.where(row >= col, both[:, :n].T, 0.0)
        result.append((lower, both[:, n:]))
    return result


def factor_kernel(per_slice, start_ref, gram_ref, high_ref, low_ref, tri_ref, basis_ref, core_ref, full, work):
    modes = full.shape[0]
    blocks = modes // BLOCK
    at = 0
    for i in range(blocks):
        for j in range(i + 1):
            block = gram_ref[at * BLOCK:(at + 1) * BLOCK, :]
            across, down = pl.ds(i * BLOCK, BLOCK), pl.ds(j * BLOCK, BLOCK)
            full[across, down] = block
            work[across, down] = block
            if j < i:
                full[down, across] = block.T
            at += 1
    tri_ref[...] = jnp.zeros_like(tri_ref)
    basis = start_ref[...].T

    def projected_gram(basis):
        projected = product(basis, full[...])
        return projected, product_nt(projected, projected)

    projected, small = projected_gram(basis)
    for i in range(max(blocks, ITERS)):
        matrices = []
        if i < blocks:
            lo = i * BLOCK
            matrices.append(work[lo:lo + BLOCK, lo:lo + BLOCK])
        if i < ITERS:
            matrices.append(small)
        factors = factor_many(matrices)
        if i < ITERS:
            basis = product(factors[-1][1], projected)
            if i + 1 < ITERS:
                projected, small = projected_gram(basis)
            else:
                basis_ref[...] = basis.T
        if i < blocks:
            lower, inverse = factors[0]
            tri_ref[lo:lo + BLOCK, lo:lo + BLOCK] = lower
            if i + 1 < blocks:
                below = product_nt(work[lo + BLOCK:, lo:lo + BLOCK], inverse)
                tri_ref[lo + BLOCK:, lo:lo + BLOCK] = below
                work[lo + BLOCK:, lo + BLOCK:] = work[lo + BLOCK:, lo + BLOCK:] - product_nt(below, below)

    b_high, b_low = split_two(basis)
    width = high_ref.shape[2]

    for c in range(high_ref.shape[0]):
        s, h = c // per_slice, c % per_slice
        high, low = high_ref[c], low_ref[c]
        value = jnp.dot(b_high, high, preferred_element_type=jnp.float32)
        value += jnp.dot(b_high, low, preferred_element_type=jnp.float32)
        value += jnp.dot(b_low, high, preferred_element_type=jnp.float32)
        core_ref[:, s, h * width:(h + 1) * width] = value


def shards(nf, ng, tensor_slab, start_matrix):
    high, low, gram = exchange_and_gram(tensor_slab, nf, ng)
    slices, cells = tensor_slab.shape[1] // nf, tensor_slab.shape[2]
    modes, rank = start_matrix.shape
    vmem = pl.BlockSpec(memory_space=pltpu.VMEM)
    triangle, basis, core = pl.pallas_call(
        functools.partial(factor_kernel, cells // high.shape[2]),
        out_shape=(
            jax.ShapeDtypeStruct((modes, modes), jnp.float32),
            jax.ShapeDtypeStruct((modes, rank), jnp.float32),
            jax.ShapeDtypeStruct((rank, slices, cells), jnp.float32),
        ),
        in_specs=[vmem] * 4,
        out_specs=(vmem, vmem, vmem),
        scratch_shapes=[pltpu.VMEM((modes, modes), jnp.float32)] * 2,
        compiler_params=pltpu.CompilerParams(vmem_limit_bytes=56 * 1024 * 1024),
    )(start_matrix, gram, high, low)
    return (triangle, basis, core)


def solution(mesh):
    placed = (P("fiber", None, "group"), P())
    return jax.shard_map(
        functools.partial(shards, mesh.shape["fiber"], mesh.shape["group"]),
        mesh=mesh,
        in_specs=placed,
        out_specs=(P(), P(), P(None, "fiber", "group")),
        check_vma=False,
    )
```

```python
import functools

import jax
import jax.numpy as jnp
from jax import lax
from jax.experimental import pallas as pl
from jax.experimental.pallas import tpu as pltpu
from jax.sharding import PartitionSpec as P

ITERS = 2
HIGHEST = lax.Precision.HIGHEST
BLOCK = 128
MESH = pl.DeviceIdType.MESH


def product(left_side, right_side):
    return jnp.dot(left_side, right_side, precision=HIGHEST, preferred_element_type=jnp.float32)


def dot_nt(a, b):
    return lax.dot_general(a, b, (((1,), (1,)), ((), ())), preferred_element_type=jnp.float32)


def split_two(value):
    high = value.astype(jnp.bfloat16)
    low = (value - high.astype(jnp.float32)).astype(jnp.bfloat16)
    return high, low


def exchange_kernel(
    nf, ng, chunks, per_slice, slices, width, rows, piece, scale,
    x_ref, high_ref, low_ref, gram_ref,
    xbuf, acc, packed, group_in, group_sum, fiber_in,
    own_sem, a_send, a_recv, g_send, g_recv, f_send, f_recv, fa_send, fa_recv, ga_send, ga_recv,
):
    mf = lax.axis_index("fiber")
    mg = lax.axis_index("group")
    barrier = pltpu.get_barrier_semaphore()
    for k in range(1, nf):
        pl.semaphore_signal(barrier, inc=1, device_id=(lax.rem(mf + k, nf), mg), device_id_type=MESH)
    for k in range(1, ng):
        pl.semaphore_signal(barrier, inc=1, device_id=(mf, lax.rem(mg + k, ng)), device_id_type=MESH)
    pl.semaphore_wait(barrier, nf + ng - 2)

    def slab_copy(c, k):
        peer = lax.rem(mf + k, nf)
        s, h = c // per_slice, c % per_slice
        return pltpu.make_async_remote_copy(
            src_ref=x_ref.at[:, peer * slices + s, pl.ds(pl.multiple_of(h * width, width), width)],
            dst_ref=xbuf.at[c, pl.ds(pl.multiple_of(mf * rows, rows), rows), :],
            send_sem=a_send.at[k - 1, c],
            recv_sem=a_recv.at[k - 1, c],
            device_id=(peer, mg),
            device_id_type=MESH,
        )

    def own_copy(c):
        s, h = c // per_slice, c % per_slice
        return pltpu.make_async_copy(
            x_ref.at[:, mf * slices + s, pl.ds(pl.multiple_of(h * width, width), width)],
            xbuf.at[c, pl.ds(pl.multiple_of(mf * rows, rows), rows), :],
            own_sem.at[c],
        )

    def start_chunk(c, _):
        for k in range(1, nf):
            slab_copy(c, k).start()
        own_copy(c).start()
        return 0

    lax.fori_loop(0, chunks, start_chunk, 0)
    acc[...] = jnp.zeros_like(acc)

    def use_chunk(c, _):
        own_copy(c).wait()
        for k in range(1, nf):
            slab_copy(c, k).wait_recv()
        high, low = split_two(xbuf[c])
        high_ref[c] = high
        low_ref[c] = low
        acc[...] += dot_nt(high, high) + (dot_nt(high, low) + dot_nt(low, high))
        return 0

    lax.fori_loop(0, chunks, use_chunk, 0)

    blocks = acc.shape[0] // BLOCK
    at = 0
    for i in range(blocks):
        for j in range(i + 1):
            packed[at * BLOCK:(at + 1) * BLOCK, :] = (
                acc[i * BLOCK:(i + 1) * BLOCK, j * BLOCK:(j + 1) * BLOCK] * scale
            )
            at += 1
    if at * BLOCK < packed.shape[0]:
        packed[at * BLOCK:, :] = jnp.zeros((packed.shape[0] - at * BLOCK, BLOCK), jnp.float32)

    big = piece * nf

    def sub_piece(q):
        return pl.multiple_of(lax.rem(mf + q, nf) * piece, 8)

    def group_copy(k, q):
        peer = lax.rem(mg + k, ng)
        return pltpu.make_async_remote_copy(
            src_ref=packed.at[pl.ds(pl.multiple_of(peer * big + sub_piece(q), 8), piece), :],
            dst_ref=group_in.at[k - 1, pl.ds(sub_piece(q), piece), :],
            send_sem=g_send.at[k - 1, q],
            recv_sem=g_recv.at[k - 1, q],
            device_id=(mf, peer),
            device_id_type=MESH,
        )

    order = list(range(1, nf)) + [0]
    for q in order:
        for k in range(1, ng):
            group_copy(k, q).start()

    def fiber_copy(k):
        peer = lax.rem(mf + k, nf)
        return pltpu.make_async_remote_copy(
            src_ref=group_sum.at[pl.ds(pl.multiple_of(peer * piece, 8), piece), :],
            dst_ref=fiber_in.at[k - 1],
            send_sem=f_send.at[k - 1],
            recv_sem=f_recv.at[k - 1],
            device_id=(peer, mg),
            device_id_type=MESH,
        )

    for q in order:
        value = packed[pl.ds(pl.multiple_of(mg * big + sub_piece(q), 8), piece), :]
        for k in range(1, ng):
            group_copy(k, q).wait_recv()
            value += group_in[k - 1, pl.ds(sub_piece(q), piece), :]
        group_sum[pl.ds(sub_piece(q), piece), :] = value
        if q:
            fiber_copy(q).start()
    total = group_sum[pl.ds(pl.multiple_of(mf * piece, 8), piece), :]
    for k in range(1, nf):
        fiber_copy(k).wait_recv()
        total += fiber_in[k - 1]
    mine = pl.ds(pl.multiple_of(mg * big + mf * piece, 8), piece)
    gram_ref[mine, :] = total

    def fiber_gather(k):
        return pltpu.make_async_remote_copy(
            src_ref=gram_ref.at[mine, :],
            dst_ref=gram_ref.at[mine, :],
            send_sem=fa_send.at[k - 1],
            recv_sem=fa_recv.at[k - 1],
            device_id=(lax.rem(mf + k, nf), mg),
            device_id_type=MESH,
        )

    def group_gather(k, q):
        part = pl.ds(pl.multiple_of(mg * big + lax.rem(mf - q + nf, nf) * piece, 8), piece)
        return pltpu.make_async_remote_copy(
            src_ref=gram_ref.at[part, :],
            dst_ref=gram_ref.at[part, :],
            send_sem=ga_send.at[k - 1, q],
            recv_sem=ga_recv.at[k - 1, q],
            device_id=(mf, lax.rem(mg + k, ng)),
            device_id_type=MESH,
        )

    for k in range(1, nf):
        fiber_gather(k).start()
    for q in range(nf):
        if q:
            fiber_gather(q).wait_recv()
        for k in range(1, ng):
            group_gather(k, q).start()
    for q in range(nf):
        for k in range(1, ng):
            group_gather(k, q).wait_recv()

    def end_chunk(c, _):
        for k in range(1, nf):
            slab_copy(c, k).wait_send()
        return 0

    lax.fori_loop(0, chunks, end_chunk, 0)
    for k in range(1, ng):
        for q in range(nf):
            group_copy(k, q).wait_send()
            group_gather(k, q).wait_send()
    for k in range(1, nf):
        fiber_copy(k).wait_send()
        fiber_gather(k).wait_send()


def exchange_and_gram(tensor_slab, nf, ng):
    rows, all_slices, cells = tensor_slab.shape
    slices = all_slices // nf
    modes = rows * nf
    width = 512 if cells % 512 == 0 else cells
    per_slice = cells // width
    chunks = slices * per_slice
    blocks = modes // BLOCK
    packed_rows = blocks * (blocks + 1) // 2 * BLOCK
    piece = -(-packed_rows // (nf * ng * 8)) * 8
    total_rows = piece * nf * ng
    scale = 1.0 / (all_slices * cells * ng)
    kernel = functools.partial(
        exchange_kernel, nf, ng, chunks, per_slice, slices, width, rows, piece, scale
    )
    dma = pltpu.SemaphoreType.DMA
    vmem = pl.BlockSpec(memory_space=pltpu.VMEM)
    high, low, gram = pl.pallas_call(
        kernel,
        out_shape=(
            jax.ShapeDtypeStruct((chunks, modes, width), jnp.bfloat16),
            jax.ShapeDtypeStruct((chunks, modes, width), jnp.bfloat16),
            jax.ShapeDtypeStruct((total_rows, BLOCK), jnp.float32),
        ),
        in_specs=[pl.BlockSpec(memory_space=pl.ANY)],
        out_specs=(vmem, vmem, vmem),
        scratch_shapes=[
            pltpu.VMEM((chunks, modes, width), jnp.float32),
            pltpu.VMEM((modes, modes), jnp.float32),
            pltpu.VMEM((total_rows, BLOCK), jnp.float32),
            pltpu.VMEM((ng - 1, piece * nf, BLOCK), jnp.float32),
            pltpu.VMEM((piece * nf, BLOCK), jnp.float32),
            pltpu.VMEM((nf - 1, piece, BLOCK), jnp.float32),
            dma((chunks,)),
            dma((nf - 1, chunks)),
            dma((nf - 1, chunks)),
            dma((ng - 1, nf)),
            dma((ng - 1, nf)),
            dma((nf - 1,)),
            dma((nf - 1,)),
            dma((nf - 1,)),
            dma((nf - 1,)),
            dma((ng - 1, nf)),
            dma((ng - 1, nf)),
        ],
        compiler_params=pltpu.CompilerParams(
            collective_id=0, has_side_effects=True, vmem_limit_bytes=56 * 1024 * 1024
        ),
    )(tensor_slab)
    return high, low, gram


def dot_tn(a, b):
    return lax.dot_general(
        a, b, (((0,), (0,)), ((), ())), precision=HIGHEST, preferred_element_type=jnp.float32
    )


def product_nt(a, b):
    return lax.dot_general(
        a, b, (((1,), (1,)), ((), ())), precision=HIGHEST, preferred_element_type=jnp.float32
    )


def factor_many(matrices):
    n = BLOCK
    row = lax.broadcasted_iota(jnp.int32, (n, n), 0)
    col = lax.broadcasted_iota(jnp.int32, (n, n), 1)
    eye = jnp.where(row == col, 1.0, 0.0).astype(jnp.float32)
    rest = [jnp.concatenate([m, eye], axis=1) for m in matrices]
    done = [[] for _ in matrices]
    for k in range(n // 8):
        panels = [w[:8] for w in rest]
        corners = [
            [jnp.broadcast_to(p[:, 8 * k + t:8 * k + t + 1], (8, n)) for t in range(8)]
            for p in panels
        ]
        rows = [[] for _ in matrices]
        for t in range(8):
            for q in range(len(matrices)):
                pivot = corners[q][t][t:t + 1]
                inverse = lax.rsqrt(pivot)
                c = corners[q][t] * inverse
                for v in range(t + 1, 8):
                    corners[q][v] = corners[q][v] - c * c[v:v + 1]
                wide = jnp.concatenate([inverse, inverse], axis=1)
                r = panels[q][t:t + 1] * wide
                rows[q].append(r)
                panels[q] = panels[q] - jnp.concatenate([c, c], axis=1) * r
        for q in range(len(matrices)):
            panel = jnp.concatenate(rows[q], axis=0)
            done[q].append(panel)
            if 8 * (k + 1) < n:
                update = dot_tn(panel[:, :n], panel)
                rest[q] = rest[q][8:] - update[8 * (k + 1):]
    result = []
    for q in range(len(matrices)):
        both = jnp.concatenate(done[q], axis=0)
        lower = jnp.where(row >= col, both[:, :n].T, 0.0)
        result.append((lower, both[:, n:]))
    return result


def factor_kernel(per_slice, start_ref, gram_ref, high_ref, low_ref, tri_ref, basis_ref, core_ref, full, work):
    modes = full.shape[0]
    blocks = modes // BLOCK
    at = 0
    for i in range(blocks):
        for j in range(i + 1):
            block = gram_ref[at * BLOCK:(at + 1) * BLOCK, :]
            across, down = pl.ds(i * BLOCK, BLOCK), pl.ds(j * BLOCK, BLOCK)
            full[across, down] = block
            work[across, down] = block
            if j < i:
                full[down, across] = block.T
            at += 1
    tri_ref[...] = jnp.zeros_like(tri_ref)
    basis = start_ref[...].T

    def projected_gram(basis):
        projected = product(basis, full[...])
        return projected, product_nt(projected, projected)

    projected, small = projected_gram(basis)
    for i in range(max(blocks, ITERS)):
        matrices = []
        if i < blocks:
            lo = i * BLOCK
            matrices.append(work[lo:lo + BLOCK, lo:lo + BLOCK])
        if i < ITERS:
            matrices.append(small)
        factors = factor_many(matrices)
        if i < ITERS:
            basis = product(factors[-1][1], projected)
            if i + 1 < ITERS:
                projected, small = projected_gram(basis)
            else:
                basis_ref[...] = basis.T
        if i < blocks:
            lower, inverse = factors[0]
            tri_ref[lo:lo + BLOCK, lo:lo + BLOCK] = lower
            if i + 1 < blocks:
                below = product_nt(work[lo + BLOCK:, lo:lo + BLOCK], inverse)
                tri_ref[lo + BLOCK:, lo:lo + BLOCK] = below
                work[lo + BLOCK:, lo + BLOCK:] = work[lo + BLOCK:, lo + BLOCK:] - product_nt(below, below)

    b_high, b_low = split_two(basis)
    width = high_ref.shape[2]

    for c in range(high_ref.shape[0]):
        s, h = c // per_slice, c % per_slice
        high, low = high_ref[c], low_ref[c]
        value = jnp.dot(b_high, high, preferred_element_type=jnp.float32)
        value += jnp.dot(b_high, low, preferred_element_type=jnp.float32)
        value += jnp.dot(b_low, high, preferred_element_type=jnp.float32)
        core_ref[:, s, h * width:(h + 1) * width] = value


def shards(nf, ng, tensor_slab, start_matrix):
    high, low, gram = exchange_and_gram(tensor_slab, nf, ng)
    slices, cells = tensor_slab.shape[1] // nf, tensor_slab.shape[2]
    modes, rank = start_matrix.shape
    vmem = pl.BlockSpec(memory_space=pltpu.VMEM)
    triangle, basis, core = pl.pallas_call(
        functools.partial(factor_kernel, cells // high.shape[2]),
        out_shape=(
            jax.ShapeDtypeStruct((modes, modes), jnp.float32),
            jax.ShapeDtypeStruct((modes, rank), jnp.float32),
            jax.ShapeDtypeStruct((rank, slices, cells), jnp.float32),
        ),
        in_specs=[vmem] * 4,
        out_specs=(vmem, vmem, vmem),
        scratch_shapes=[pltpu.VMEM((modes, modes), jnp.float32)] * 2,
        compiler_params=pltpu.CompilerParams(vmem_limit_bytes=56 * 1024 * 1024),
    )(start_matrix, gram, high, low)
    return (triangle, basis, core)


def solution(mesh):
    placed = (P("fiber", None, "group"), P())
    return jax.shard_map(
        functools.partial(shards, mesh.shape["fiber"], mesh.shape["group"]),
        mesh=mesh,
        in_specs=placed,
        out_specs=(P(), P(), P(None, "fiber", "group")),
        check_vma=False,
    )
```
